256 devices in a mesh: dp: 8 (over y, z_hi), row: 4 (over z_lo), col: 8 (over x, core).
Axes of the slice: x: 4, y: 4, z: 8 (z_hi: 2, z_lo: 4; z = z_hi * 4 + z_lo), core: 2. Of those that a mesh axis runs over, the one named last changes fastest.
Arguments:
- pre_act: bfloat16 [4096, 24576], P(('dp', 'row'), 'col'), may hold values from -6 to 6
- grad_out: bfloat16 [4096, 6144], P(('dp', 'col'), 'row'), may hold values from -6 to 6
- down_weight: bfloat16 [24576, 6144], P('col', 'row'), may hold values from -0.078125 to 0.078125
Outputs:
- grad_pre: bfloat16 [4096, 24576], P(('dp', 'row'), 'col')
- grad_down: float32 [24576, 6144], P(('col', 'dp'), 'row')
The draws below stay inside these ranges and needn't reach their ends.
All inputs are finite; a program needn't handle non-finite values.
Results may differ from the reference program's by a relative error of at most 0.0027.
Values may be sent and summed in bfloat16 or wider, within the bound.
No kernel may reach another device: no remote copies, remote signals or barrier semaphores. Data moves between devices by JAX's collectives and lax.ppermute only.
A program may use at most 128 MiB of HBM per device.

```python
import math
import jax
import jax.numpy as jnp

D = 6144
FF = 24576
TOKENS = 4096


def block_levels(rng, shape, pieces, least, largest):
    factor_of = 1.0
    for position, shards_of in pieces:
        draws = jax.random.uniform(jax.random.fold_in(jax.random.fold_in(rng, 6), position), (shards_of,), jnp.float32, least / len(pieces), largest / len(pieces))
        factor_of = factor_of * jnp.repeat(jnp.exp(draws), shape[position] // shards_of).reshape((-1,) + (1,) * (len(shape) - 1 - position))
    return factor_of


def gaussian(stream_key, shape, deviation, most, cuts=(), dtype=jnp.bfloat16):
    level = block_levels(stream_key, shape, cuts, -0.22, 0.18) if cuts else 1.0
    result = jax.random.normal(stream_key, shape, jnp.float32) * deviation * level
    return jnp.minimum(jnp.maximum(result, -most), most).astype(dtype)


def setup_inputs(seed: int = 0) -> dict:
    seeds = jax.random.split(jax.random.key(seed), 4)
    return {
        "pre_act": gaussian(seeds[0], (TOKENS, FF), 1.5, 6.0, ((0, 32), (1, 8))),
        "grad_out": gaussian(seeds[1], (TOKENS, D), 1.0, 6.0, ((0, 64), (1, 4))),
        "down_weight": gaussian(seeds[2], (FF, D), D ** -0.5, 0.078125, ((0, 8), (1, 4))),
    }


root_two_pi = math.sqrt(2.0 / math.pi)
gelu_coeff = 0.044715

def gelu_parts(pre_values):
    cubic_term = gelu_coeff * pre_values * pre_values * pre_values
    inner_arg = root_two_pi * (pre_values + cubic_term)
    tangent = jnp.tanh(inner_arg)
    gelu_value = 0.5 * pre_values * (1.0 + tangent)
    gelu_slope = 0.5 * (1.0 + tangent) + 0.5 * pre_values * (1.0 - tangent * tangent) * root_two_pi * (1.0 + 3.0 * gelu_coeff * pre_values * pre_values)
    return (gelu_value, gelu_slope)

def reference(pre_act, grad_out, down_weight):
    pre_float = pre_act.astype(jnp.float32)
    gelu_value, gelu_slope = gelu_parts(pre_float)
    activation = gelu_value.astype(jnp.bfloat16)
    grad_float = grad_out.astype(jnp.float32)
    grad_act = jnp.dot(grad_float, down_weight.astype(jnp.float32).T, preferred_element_type=jnp.float32)
    grad_pre = (grad_act * gelu_slope).astype(jnp.bfloat16)
    grad_down = jnp.dot(activation.astype(jnp.float32).T, grad_float, preferred_element_type=jnp.float32)
    grad_down = grad_down * (1.0 / math.sqrt(TOKENS))
    return (grad_pre, grad_down)
```

```python
import math

import jax
import jax.numpy as jnp
from jax import lax
from jax.sharding import Mesh
from jax.sharding import PartitionSpec as P

root_two_pi = math.sqrt(2.0 / math.pi)
gelu_coeff = 0.044715
Z = ("zh", "zl")


def gelu_parts(pre_values):
    cubic_term = gelu_coeff * pre_values * pre_values * pre_values
    inner_arg = root_two_pi * (pre_values + cubic_term)
    tangent = jnp.tanh(inner_arg)
    gelu_value = 0.5 * pre_values * (1.0 + tangent)
    gelu_slope = 0.5 * (1.0 + tangent) + 0.5 * pre_values * (
        1.0 - tangent * tangent
    ) * root_two_pi * (1.0 + 3.0 * gelu_coeff * pre_values * pre_values)
    return (gelu_value, gelu_slope)


def shift(v, axis, step):
    n = lax.axis_size(axis)
    return lax.ppermute(v, axis, [(i, (i + step) % n) for i in range(n)])


def along_z(v, step, senders):
    pairs = [(4 * h + l, (4 * h + l + step) % 8) for h in range(2) for l in senders]
    return lax.ppermute(v, Z, pairs)


def at(v, i):
    return lax.dynamic_index_in_dim(v, i, 0, keepdims=False)


def swap_halves(v, flag):
    h = v.shape[0] // 2
    return jnp.where(flag, jnp.concatenate([v[h:], v[:h]]), v)


def pack(v):
    top = jnp.max(jnp.abs(v), axis=1, keepdims=True)
    e = jnp.clip(jnp.floor(jnp.log2(jnp.maximum(top, 1e-30))), -100.0, 100.0)
    body = (v * jnp.exp2(13.0 - e)).astype(jnp.float16)
    tail = jnp.broadcast_to(e, (v.shape[0], 128)).astype(jnp.float16)
    return jnp.concatenate([body, tail], axis=1)


def unpack(w):
    n = w.shape[1] - 128
    e = w[:, n : n + 1].astype(jnp.float32)
    return w[:, :n].astype(jnp.float32) * jnp.exp2(e - 13.0)


def on_device(pre_act, grad_out, down_weight):
    y, zh, zl, x, c = (lax.axis_index(a) for a in ("y", "zh", "zl", "x", "core"))
    j = zh * 4 + zl
    tokens, hidden = pre_act.shape
    half, feats = grad_out.shape
    block = hidden // 8
    grad_scale = 1.0 / math.sqrt(tokens * 32)

    pre = swap_halves(pre_act, c == 1).astype(jnp.float32)
    gelu_value, gelu_slope = gelu_parts(pre)
    act = gelu_value.astype(jnp.bfloat16).reshape(tokens, 4, 2, block).transpose(1, 2, 0, 3)
    act = jnp.where(zh == 1, act[:, ::-1], act)
    pieces = [at(act, (y + s) % 4) for s in range(4)]
    pieces = [pieces[0]] + [shift(pieces[s], "y", s) for s in range(1, 4)]
    own = jnp.concatenate([v[0] for v in pieces])
    cross = jnp.concatenate([v[1] for v in pieces])

    g = grad_out
    p = shift(g, "zh", 1)
    ga = jnp.zeros((4, half, feats), g.dtype)
    for t in range(4):
        ga = lax.dynamic_update_index_in_dim(ga, shift(g, "x", t) if t else g, (x - t) % 4, 0)
    ga_o = shift(ga, "core", 1)
    q = jnp.where(jnp.where(zl == 0, x == 3, x == 0), p, jnp.zeros_like(p))
    for t in (1, 2, 3):
        pairs = [(3, (3 + t) % 4), (12, 12 + t)]
        q = q + lax.ppermute(p, ("zl", "x"), pairs)
    q_o = shift(q, "core", 1)
    pc = jnp.stack([p] + [shift(p, "y", s) for s in range(1, 4)])

    mine = jnp.stack([ga, ga_o], axis=1).reshape(4, tokens, feats)
    beyond = jnp.concatenate([q, q_o])
    edge = jnp.where(zl == 0, 3, 0)
    takes = jnp.logical_and(jnp.arange(4) == edge, jnp.logical_or(zl == 0, zl == 3))
    rows = jnp.where(takes[:, None, None], beyond[None], mine)
    partial = lax.dot_general(
        rows.reshape(4 * tokens, feats),
        down_weight,
        (((1,), (1,)), ((), ())),
        preferred_element_type=jnp.float32,
    ).reshape(4, tokens, hidden)
    up = at(partial, (zl + 1) % 4)
    down = at(partial, (zl + 3) % 4)
    far = pack(at(partial, (zl + 2) % 4))
    far_up = along_z(far, 1, (0, 1))
    far_down = along_z(far, -1, (2, 3))
    from_below = along_z(pack(up + unpack(far_up)), 1, range(4))
    from_above = along_z(pack(down + unpack(far_down)), -1, range(4))
    grad_act = at(partial, zl) + unpack(from_below) + unpack(from_above)
    grad_pre = swap_halves((grad_act * gelu_slope).astype(jnp.bfloat16), c == 1)

    r = [None] * 7
    l = [None] * 7
    r[1] = along_z(jnp.where(zl < 2, own, cross), 1, range(4))
    l[1] = along_z(jnp.where(zl < 2, cross, own), -1, range(4))
    r[2] = along_z(jnp.where(zl == 2, own, r[1]), 1, range(4))
    l[2] = along_z(jnp.where(zl == 1, own, l[1]), -1, range(4))
    r[3] = along_z(jnp.where(zl == 2, r[1], r[2]), 1, (0, 1, 2))
    l[3] = along_z(jnp.where(zl == 1, l[1], l[2]), -1, (1, 2, 3))
    r[4] = along_z(jnp.where(zl == 2, r[2], r[3]), 1, (1, 2))
    l[4] = along_z(jnp.where(zl == 1, l[2], l[3]), -1, (1, 2))
    r[5] = along_z(r[3], 1, (2,))
    l[5] = along_z(l[3], -1, (1,))
    r[6] = along_z(r[4], 1, (2,))
    l[6] = along_z(l[4], -1, (1,))

    gg = jnp.zeros((2, 4, 4, 2, half, feats), g.dtype)
    for s in range(4):
        b = shift(ga, "y", s) if s else ga
        for o in range(2):
            v = b if o == 0 else (shift(b, "core", 1) if s else ga_o)
            gg = lax.dynamic_update_slice(gg, v[None, :, None, None], (zh, 0, s, o, 0, 0))
    for t in range(4):
        d = shift(pc, "x", t) if t else pc
        for o in range(2):
            v = d if o == 0 else shift(d, "core", 1)
            gg = lax.dynamic_update_slice(gg, v[None, None, :, None], (1 - zh, (x - t) % 4, 0, o, 0, 0))
    gg = gg.reshape(8, 4 * tokens, feats)

    def product(unit, source):
        return lax.dot_general(
            unit, at(gg, source % 8), (((0,), (0,)), ((), ())), preferred_element_type=jnp.float32
        )

    r_at = [j - k + jnp.where(zl == 3, 1, 0) for k in range(7)]
    l_at = [j + k - jnp.where(zl == 0, 1, 0) for k in range(7)]
    summed = product(own, j)
    summed += product(jnp.where(zl == 3, 0, r[1]), r_at[1])
    summed += product(jnp.where(zl == 0, 0, l[1]), l_at[1])
    summed += product(r[2], r_at[2])
    summed += product(l[2], l_at[2])
    summed += product(r[3], r_at[3])
    summed += product(l[3], l_at[3])
    for k in (4, 5, 6):
        summed += product(jnp.where(zl > 1, r[k], l[k]), jnp.where(zl > 1, r_at[k], l_at[k]))
    return (grad_pre, summed * grad_scale)


def solution(mesh):
    axes = ("y", "zh", "zl", "x", "core")
    fine = Mesh(mesh.devices.reshape(4, 2, 4, 4, 2), axes)
    dp, row, col = ("y", "zh"), "zl", ("x", "core")
    return jax.shard_map(
        on_device,
        mesh=fine,
        in_specs=(P((*dp, row), col), P((*dp, *col), row), P(col, row)),
        out_specs=(P((*dp, row), col), P((*col, *dp), row)),
        check_vma=False,
    )
```

```python
import math

import jax
import jax.numpy as jnp
from jax import lax
from jax.sharding import Mesh
from jax.sharding import PartitionSpec as P

root_two_pi = math.sqrt(2.0 / math.pi)
gelu_coeff = 0.044715
Z = ("zh", "zl")


def gelu_parts(pre_values):
    cubic_term = gelu_coeff * pre_values * pre_values * pre_values
    inner_arg = root_two_pi * (pre_values + cubic_term)
    tangent = jnp.tanh(inner_arg)
    gelu_value = 0.5 * pre_values * (1.0 + tangent)
    gelu_slope = 0.5 * (1.0 + tangent) + 0.5 * pre_values * (
        1.0 - tangent * tangent
    ) * root_two_pi * (1.0 + 3.0 * gelu_coeff * pre_values * pre_values)
    return (gelu_value, gelu_slope)


def shift(v, axis, step):
    n = lax.axis_size(axis)
    return lax.ppermute(v, axis, [(i, (i + step) % n) for i in range(n)])


def along_z(v, step, senders):
    pairs = [(4 * h + l, (4 * h + l + step) % 8) for h in range(2) for l in senders]
    return lax.ppermute(v, Z, pairs)


def at(v, i):
    return lax.dynamic_index_in_dim(v, i, 0, keepdims=False)


def after(v, *first):
    return lax.optimization_barrier((v, *first))[0]


def pack(v):
    top = jnp.max(jnp.abs(v), axis=1, keepdims=True)
    e = jnp.clip(jnp.floor(jnp.log2(jnp.maximum(top, 1e-30))), -100.0, 100.0)
    body = (v * jnp.exp2(13.0 - e)).astype(jnp.float16)
    tail = jnp.broadcast_to(e, (v.shape[0], 128)).astype(jnp.float16)
    return jnp.concatenate([body, tail], axis=1)


def unpack(w):
    n = w.shape[1] - 128
    e = w[:, n : n + 1].astype(jnp.float32)
    return w[:, :n].astype(jnp.float32) * jnp.exp2(e - 13.0)


def on_device(pre_act, grad_out, down_weight):
    y, zh, zl, x, c = (lax.axis_index(a) for a in ("y", "zh", "zl", "x", "core"))
    j = zh * 4 + zl
    tokens, hidden = pre_act.shape
    half, feats = grad_out.shape
    block = hidden // 8
    grad_scale = 1.0 / math.sqrt(tokens * 32)

    g = grad_out
    p = shift(g, "zh", 1)
    g_all = lax.all_gather(g, ("x", "y"))
    p_all = lax.all_gather(p, ("x", "y"))
    g_from = [g] + [shift(g, "x", t) for t in (1, 2, 3)]

    gelu_value, gelu_slope = gelu_parts(pre_act.astype(jnp.float32))
    act = gelu_value.astype(jnp.bfloat16).reshape(tokens, 4, 2, block).transpose(1, 2, 0, 3)
    act = jnp.where(zh == 1, act[:, ::-1], act)
    halves = act.reshape(4, 2, 2, half, block)
    act = jnp.where(c == 1, halves[:, :, ::-1], halves)
    pieces_out = [at(act, (y + s) % 4) for s in range(4)]
    pieces = [shift(v, "y", s) if s else v for s, v in enumerate(pieces_out)]
    own, cross = (
        jnp.stack([lax.select_n((y - k) % 4, *[v[i] for v in pieces]) for k in range(4)], axis=1)
        for i in range(2)
    )

    ga = after(jnp.stack(g_from), *pieces_out)
    ga_o = shift(ga, "core", 1)
    q = jnp.where(jnp.where(zl == 0, x == 3, x == 0), p, jnp.zeros_like(p))
    for t in (1, 2, 3):
        pairs = [(3, (3 + t) % 4), (12, 12 + t)]
        q = q + lax.ppermute(p, ("zl", "x"), pairs)
    q_o = shift(q, "core", 1)
    mine = jnp.stack([ga, ga_o], axis=1)
    beyond = jnp.stack([q, q_o])

    mine = after(mine, own, cross)

    def partial(k):
        v = at(mine, (x - zl - k) % 4)
        if k == 1:
            v = jnp.where(zl == 3, beyond, v)
        if k == -1:
            v = jnp.where(zl == 0, beyond, v)
        v = jnp.where(c == 1, v[::-1], v).reshape(tokens, feats)
        return lax.dot_general(
            v, down_weight, (((1,), (1,)), ((), ())), preferred_element_type=jnp.float32
        )

    r1 = along_z(jnp.where(zl < 2, own, cross), 1, range(4))
    l1 = along_z(jnp.where(zl < 2, cross, own), -1, range(4))
    far = pack(partial(2))
    far_up = along_z(far, 1, (0, 1))
    far_down = along_z(far, -1, (2, 3))
    r2 = along_z(jnp.where(zl == 2, own, r1), 1, range(4))
    l2 = along_z(jnp.where(zl == 1, own, l1), -1, range(4))
    from_below = along_z(pack(partial(1) + unpack(far_up)), 1, range(4))
    from_above = along_z(pack(partial(-1) + unpack(far_down)), -1, range(4))
    r3 = along_z(after(jnp.where(zl == 2, r1, r2), g_all), 1, (0, 1, 2))
    l3 = along_z(after(jnp.where(zl == 1, l1, l2), g_all), -1, (3, 2, 1))
    r4 = along_z(jnp.where(zl == 2, r2, r3), 1, (1, 2))
    l4 = along_z(jnp.where(zl == 1, l2, l3), -1, (2, 1))
    r5 = along_z(r3, 1, (2,))
    l5 = along_z(l3, -1, (1,))
    r6 = along_z(after(r4, p_all), 1, (2,))
    l6 = along_z(after(l4, p_all), -1, (1,))

    mid = partial(0)
    grad_act = mid + unpack(from_below) + unpack(from_above)
    grad_pre = (grad_act * gelu_slope).astype(jnp.bfloat16)

    g_all = after(g_all, r3, l3).reshape(4, 4, half, feats)
    g_both = (g_all, shift(g_all, "core", 1))
    p_all = after(p_all, r5, l5).reshape(4, 4, half, feats)
    p_both = (p_all, shift(p_all, "core", 1))

    def product(unit, both, source):
        return sum(
            lax.dot_general(
                unit[o].reshape(4 * half, block),
                at(both[o], source).reshape(4 * half, feats),
                (((0,), (0,)), ((), ())),
                preferred_element_type=jnp.float32,
            )
            for o in range(2)
        )

    def choose(*units):
        return lax.select_n(zl, *units)

    r1, r2, r3, r4, r5, l1, l2, l3, l4, l5 = lax.optimization_barrier(
        (r1, r2, r3, r4, r5, l1, l2, l3, l4, l5)
    )
    summed = product(own, g_both, zl)
    summed += product(choose(l4, r1, r1, r2), g_both, (zl + 3) % 4)
    summed += product(choose(l2, l1, l1, r4), g_both, (zl + 1) % 4)
    summed += product(choose(l3, l2, r2, r3), g_both, (zl + 2) % 4)
    low = zl < 2
    summed += product(choose(r1, r2, l2, l1), p_both, jnp.where(low, 3, 0))
    summed += product(choose(r2, r3, l3, l2), p_both, jnp.where(low, 2, 1))
    summed += product(choose(l5, l3, r3, r5), p_both, jnp.where(low, 0, 3))
    summed += product(choose(l6, l4, r4, r6), p_both, jnp.where(low, 1, 2))
    return (grad_pre, summed * grad_scale)


def solution(mesh):
    axes = ("y", "zh", "zl", "x", "core")
    fine = Mesh(mesh.devices.reshape(4, 2, 4, 4, 2), axes)
    dp, row, col = ("y", "zh"), "zl", ("x", "core")
    return jax.shard_map(
        on_device,
        mesh=fine,
        in_specs=(P((*dp, row), col), P((*dp, *col), row), P(col, row)),
        out_specs=(P((*dp, row), col), P((*col, *dp), row)),
        check_vma=False,
    )
```

```python
import math

import jax
import jax.numpy as jnp
from jax import lax
from jax.sharding import Mesh
from jax.sharding import PartitionSpec as P

root_two_pi = math.sqrt(2.0 / math.pi)
gelu_coeff = 0.044715
Z = ("zh", "zl")


def gelu_parts(pre_values):
    cubic_term = gelu_coeff * pre_values * pre_values * pre_values
    inner_arg = root_two_pi * (pre_values + cubic_term)
    tangent = jnp.tanh(inner_arg)
    gelu_value = 0.5 * pre_values * (1.0 + tangent)
    gelu_slope = 0.5 * (1.0 + tangent) + 0.5 * pre_values * (
        1.0 - tangent * tangent
    ) * root_two_pi * (1.0 + 3.0 * gelu_coeff * pre_values * pre_values)
    return (gelu_value, gelu_slope)


def shift(v, axis, step):
    n = lax.axis_size(axis)
    return lax.ppermute(v, axis, [(i, (i + step) % n) for i in range(n)])


def along_z(v, step, senders):
    pairs = [(4 * h + l, (4 * h + l + step) % 8) for h in range(2) for l in senders]
    return lax.ppermute(v, Z, pairs)


def at(v, i):
    return lax.dynamic_index_in_dim(v, i, 0, keepdims=False)


def after(v, *first):
    return lax.optimization_barrier((v, *first))[0]


def pack(v):
    top = jnp.max(jnp.abs(v), axis=1, keepdims=True)
    e = jnp.clip(jnp.floor(jnp.log2(jnp.maximum(top, 1e-30))), -100.0, 100.0)
    body = (v * jnp.exp2(13.0 - e)).astype(jnp.float16)
    tail = jnp.broadcast_to(e, (v.shape[0], 128)).astype(jnp.float16)
    return jnp.concatenate([body, tail], axis=1)


def unpack(w):
    n = w.shape[1] - 128
    e = w[:, n : n + 1].astype(jnp.float32)
    return w[:, :n].astype(jnp.float32) * jnp.exp2(e - 13.0)


def on_device(pre_act, grad_out, down_weight):
    y, zh, zl, x, c = (lax.axis_index(a) for a in ("y", "zh", "zl", "x", "core"))
    j = zh * 4 + zl
    tokens, hidden = pre_act.shape
    half, feats = grad_out.shape
    block = hidden // 8
    grad_scale = 1.0 / math.sqrt(tokens * 32)

    g = grad_out
    p = shift(g, "zh", 1)
    g_from = [g] + [shift(g, "x", t) for t in (1, 2, 3)]
    all_rows = lax.all_gather(jnp.stack([g, p]), ("x", "y")).reshape(4, 4, 2, half, feats)

    gelu_value, gelu_slope = gelu_parts(pre_act.astype(jnp.float32))
    act, gelu_slope = lax.optimization_barrier((gelu_value.astype(jnp.bfloat16), gelu_slope))
    act = act.reshape(tokens, 4, 2, block).transpose(1, 2, 0, 3)
    act = jnp.where(zh == 1, act[:, ::-1], act)
    halves = act.reshape(4, 2, 2, half, block)
    act = jnp.where(c == 1, halves[:, :, ::-1], halves)
    pieces_out = [at(act, (y + s) % 4) for s in range(4)]
    pieces = [shift(v, "y", s) if s else v for s, v in enumerate(pieces_out)]
    own, cross = (
        jnp.stack([lax.select_n((y - k) % 4, *[v[i] for v in pieces]) for k in range(4)], axis=1)
        for i in range(2)
    )

    ga = after(jnp.stack(g_from), *pieces_out)
    ga_o = shift(ga, "core", 1)
    q = jnp.where(jnp.where(zl == 0, x == 3, x == 0), p, jnp.zeros_like(p))
    for t in (1, 2, 3):
        pairs = [(3, (3 + t) % 4), (12, 12 + t)]
        q = q + lax.ppermute(p, ("zl", "x"), pairs)
    q_o = shift(q, "core", 1)
    mine = after(jnp.stack([ga, ga_o], axis=1), own, cross)
    beyond = jnp.stack([q, q_o])

    rows = [at(mine, (x - zl - k) % 4) for k in (2, 1, -1, 0)]
    rows[1] = jnp.where(zl == 3, beyond, rows[1])
    rows[2] = jnp.where(zl == 0, beyond, rows[2])
    rows = jnp.stack(rows)
    rows = jnp.where(c == 1, rows[:, ::-1], rows).reshape(4 * tokens, feats)
    parts = lax.dot_general(
        rows, down_weight, (((1,), (1,)), ((), ())), preferred_element_type=jnp.float32
    )
    part_far, part_up, part_down, part_own = (
        parts[k * tokens : (k + 1) * tokens] for k in range(4)
    )
    far = pack(part_far)

    r1 = along_z(jnp.where(zl < 2, own, cross), 1, range(4))
    l1 = along_z(jnp.where(zl < 2, cross, own), -1, range(4))
    r2 = along_z(jnp.where(zl == 2, own, r1), 1, range(4))
    l2 = along_z(jnp.where(zl == 1, own, l1), -1, range(4))
    far = after(far, r2, l2)
    far_up = along_z(far, 1, (0, 1))
    far_down = along_z(far, -1, (2, 3))
    r3 = along_z(jnp.where(zl == 2, r1, r2), 1, (0, 1, 2))
    l3 = along_z(jnp.where(zl == 1, l1, l2), -1, (3, 2, 1))
    r4 = along_z(after(jnp.where(zl == 2, r2, r3), far), 1, (1, 2))
    l4 = along_z(after(jnp.where(zl == 1, l2, l3), far), -1, (2, 1))
    r5 = along_z(after(r3, far), 1, (2,))
    l5 = along_z(after(l3, far), -1, (1,))
    near_up = pack(part_up + unpack(after(far_up, r3, l3)))
    near_down = pack(part_down + unpack(after(far_down, r3, l3)))
    from_below = along_z(near_up, 1, range(4))
    from_above = along_z(near_down, -1, range(4))
    r6 = along_z(r4, 1, (2,))
    l6 = along_z(l4, -1, (1,))

    all_rows = after(all_rows, near_up, near_down)
    other_rows = shift(all_rows, "core", 1)
    own, r1, r2, r3, r4, r5, l1, l2, l3, l4, l5 = lax.optimization_barrier(
        (own, r1, r2, r3, r4, r5, l1, l2, l3, l4, l5)
    )

    def choose(*units):
        return lax.select_n(zl, *units)

    none = jnp.zeros_like(own)
    in_group = (
        choose(own, r1, r2, r4),
        choose(l2, own, r1, r3),
        choose(l3, l1, own, r2),
        choose(l4, l2, l1, own),
    )
    from_group = (
        choose(l5, l3, l2, l1),
        choose(none, l4, l3, l2),
        choose(r2, r3, r4, none),
        choose(r1, r2, r3, r5),
    )
    units = [jnp.stack([a, b], axis=2) for a, b in zip(in_group, from_group)]
    last = choose(l6, none, none, r6)
    last = jnp.stack([jnp.zeros_like(last), last], axis=2)

    def product(unit, rows):
        return lax.dot_general(
            unit.reshape(-1, block), rows.reshape(-1, feats), (((0,), (0,)), ((), ())),
            preferred_element_type=jnp.float32,
        )

    summed = 0.0
    for k in (0, 2):
        summed += product(jnp.stack([units[k][0], units[k + 1][0]]), all_rows[k : k + 2])
    for k in (0, 2):
        summed += product(jnp.stack([units[k][1], units[k + 1][1]]), other_rows[k : k + 2])
    low = zl < 2
    summed += product(last[0], at(all_rows, jnp.where(low, 1, 2)))
    summed += product(last[1], at(other_rows, jnp.where(low, 1, 2)))

    grad_act = part_own + unpack(from_below) + unpack(from_above)
    grad_pre = (grad_act * gelu_slope).astype(jnp.bfloat16)
    return (grad_pre, summed * grad_scale)


def solution(mesh):
    axes = ("y", "zh", "zl", "x", "core")
    fine = Mesh(mesh.devices.reshape(4, 2, 4, 4, 2), axes)
    dp, row, col = ("y", "zh"), "zl", ("x", "core")
    return jax.shard_map(
        on_device,
        mesh=fine,
        in_specs=(P((*dp, row), col), P((*dp, *col), row), P(col, row)),
        out_specs=(P((*dp, row), col), P((*col, *dp), row)),
        check_vma=False,
    )
```

```python
import math

import jax
import jax.numpy as jnp
from jax import lax
from jax.sharding import Mesh
from jax.sharding import PartitionSpec as P

root_two_pi = math.sqrt(2.0 / math.pi)
gelu_coeff = 0.044715
Z = ("zh", "zl")


def gelu_parts(pre_values):
    cubic_term = gelu_coeff * pre_values * pre_values * pre_values
    inner_arg = root_two_pi * (pre_values + cubic_term)
    tangent = jnp.tanh(inner_arg)
    gelu_value = 0.5 * pre_values * (1.0 + tangent)
    gelu_slope = 0.5 * (1.0 + tangent) + 0.5 * pre_values * (
        1.0 - tangent * tangent
    ) * root_two_pi * (1.0 + 3.0 * gelu_coeff * pre_values * pre_values)
    return (gelu_value, gelu_slope)


def shift(v, axis, step):
    n = lax.axis_size(axis)
    return lax.ppermute(v, axis, [(i, (i + step) % n) for i in range(n)])


def along_z(v, step, senders):
    pairs = [(4 * h + l, (4 * h + l + step) % 8) for h in range(2) for l in senders]
    return lax.ppermute(v, Z, pairs)


def pairs_z(v, steps):
    pairs = [(4 * h + l, (4 * h + l + s) % 8) for h in range(2) for l, s in steps.items()]
    return lax.ppermute(v, Z, pairs)


def at(v, i):
    return lax.dynamic_index_in_dim(v, i, 0, keepdims=False)


def after(v, *first):
    return lax.optimization_barrier((v, *first))[0]


def pack(v):
    top = jnp.max(jnp.abs(v), axis=1, keepdims=True)
    e = jnp.clip(jnp.floor(jnp.log2(jnp.maximum(top, 1e-30))), -100.0, 100.0)
    body = (v * jnp.exp2(13.0 - e)).astype(jnp.float16)
    tail = jnp.broadcast_to(e, (v.shape[0], 128)).astype(jnp.float16)
    return jnp.concatenate([body, tail], axis=1)


def unpack(w):
    n = w.shape[1] - 128
    e = w[:, n : n + 1].astype(jnp.float32)
    return w[:, :n].astype(jnp.float32) * jnp.exp2(e - 13.0)


def on_device(pre_act, grad_out, down_weight):
    y, zh, zl, x, c = (lax.axis_index(a) for a in ("y", "zh", "zl", "x", "core"))
    tokens, hidden = pre_act.shape
    half, feats = grad_out.shape
    block = hidden // 8
    grad_scale = 1.0 / math.sqrt(tokens * 32)

    p = shift(grad_out, "zh", 1)
    gelu_value, gelu_slope = gelu_parts(pre_act.astype(jnp.float32))
    act, gelu_slope = lax.optimization_barrier((gelu_value.astype(jnp.bfloat16), gelu_slope))
    act = act.reshape(tokens, 4, 2, block).transpose(1, 2, 0, 3)
    act = jnp.where(zh == 1, act[:, ::-1], act)
    halves = act.reshape(4, 2, 2, half, block)
    act = jnp.where(c == 1, halves[:, :, ::-1], halves)
    pieces_out = [at(act, (y + s) % 4) for s in range(4)]
    pieces = [shift(v, "y", s) if s else v for s, v in enumerate(pieces_out)]
    own, cross = (
        jnp.stack([lax.select_n((y - k) % 4, *[v[i] for v in pieces]) for k in range(4)], axis=1)
        for i in range(2)
    )

    both = after(jnp.stack([grad_out, p]), *pieces_out)
    all_rows = lax.all_gather(both, ("x", "y")).reshape(4, 4, 2, half, feats)

    from_x = jnp.stack([both] + [shift(both, "x", t) for t in (1, 2, 3)])
    beyond = at(from_x[:, 1], jnp.where(zl == 0, x - 3, x) % 4)
    mine = jnp.concatenate([from_x[:, 0], beyond[None]])
    mine = jnp.stack([mine, shift(mine, "core", 1)], axis=1)
    mine = after(mine, own, cross)

    place = [(x - zl - k) % 4 for k in (2, 1, -1, 0)]
    place[1] = jnp.where(zl == 3, 4, place[1])
    place[2] = jnp.where(zl == 0, 4, place[2])
    rows = jnp.stack([at(mine, k) for k in place])
    rows = jnp.where(c == 1, rows[:, ::-1], rows).reshape(4 * tokens, feats)
    parts = lax.dot_general(
        rows, down_weight, (((1,), (1,)), ((), ())), preferred_element_type=jnp.float32
    )
    part_far, part_up, part_down, part_own = (
        parts[k * tokens : (k + 1) * tokens] for k in range(4)
    )
    far = pack(part_far)

    e0, e3 = zl == 0, zl == 3
    a_up = along_z(jnp.where(e3, cross, own), 1, range(4))
    a_down = along_z(jnp.where(e0, cross, own), -1, range(4))
    b = pairs_z(cross, {0: -2, 1: -2, 2: 2, 3: 2})
    far_up = along_z(far, 1, (0, 1))
    far_down = along_z(far, -1, (2, 3))
    c_up = along_z(after(jnp.where(e0, b, a_up), far), 1, (0, 1, 2))
    c_down = along_z(after(jnp.where(e3, b, a_down), far), -1, (3, 2, 1))
    d = pairs_z(after(b, far), {1: 1, 2: -1})
    near_up = pack(part_up + unpack(after(far_up, a_up, a_down, b)))
    near_down = pack(part_down + unpack(after(far_down, a_up, a_down, b)))
    from_below = along_z(near_up, 1, range(4))
    from_above = along_z(near_down, -1, range(4))
    e = pairs_z(jnp.where(zl == 1, c_up, c_down), {1: 1, 2: -1})
    f = pairs_z(jnp.where(zl == 2, c_up, c_down), {1: -1, 2: 1})
    g = pairs_z(d, {1: -1, 2: 1})
    h = pairs_z(e, {1: -1, 2: 1})

    all_rows = after(all_rows, e, f, g)
    other_rows = shift(all_rows, "core", 1)
    own, a_up, a_down, b, c_up, c_down, d, e, f, g = lax.optimization_barrier(
        (own, a_up, a_down, b, c_up, c_down, d, e, f, g)
    )

    def choose(*units):
        return lax.select_n(zl, *units)

    in_group = (
        choose(own, a_up, c_up, f),
        choose(a_down, own, a_up, c_up),
        choose(c_down, a_down, own, a_up),
        choose(f, c_down, a_down, own),
    )
    from_group = (
        choose(g, d, b, a_down),
        choose(h, e, c_down, b),
        choose(b, c_up, e, h),
        choose(a_up, b, d, g),
    )
    none = jnp.zeros_like(own)
    early = (from_group[0], choose(none, e, c_down, b), choose(b, c_up, e, none), from_group[3])
    last = choose(h, none, none, h)

    def product(core, first, second, rows):
        unit = jnp.stack([jnp.stack([i[core], j[core]], axis=1) for i, j in zip(first, second)])
        return lax.dot_general(
            unit.reshape(-1, block), rows.reshape(-1, feats), (((0,), (0,)), ((), ())),
            preferred_element_type=jnp.float32,
        )

    summed = product(0, in_group, early, all_rows)
    from_below, from_above = after(from_below, summed), after(from_above, summed)
    summed += product(0, (none,), (last,), at(all_rows, jnp.where(zl < 2, 1, 2)))
    summed += product(1, in_group, from_group, other_rows)

    grad_act = part_own + unpack(from_below) + unpack(from_above)
    grad_pre = (grad_act * gelu_slope).astype(jnp.bfloat16)
    return (grad_pre, summed * grad_scale)


def solution(mesh):
    axes = ("y", "zh", "zl", "x", "core")
    fine = Mesh(mesh.devices.reshape(4, 2, 4, 4, 2), axes)
    dp, row, col = ("y", "zh"), "zl", ("x", "core")
    return jax.shard_map(
        on_device,
        mesh=fine,
        in_specs=(P((*dp, row), col), P((*dp, *col), row), P(col, row)),
        out_specs=(P((*dp, row), col), P((*col, *dp), row)),
        check_vma=False,
    )
```

```python
import math

import jax
import jax.numpy as jnp
from jax import lax
from jax.sharding import Mesh
from jax.sharding import PartitionSpec as P

root_two_pi = math.sqrt(2.0 / math.pi)
gelu_coeff = 0.044715
Z = ("zh", "zl")


def gelu_parts(pre_values):
    cubic_term = gelu_coeff * pre_values * pre_values * pre_values
    inner_arg = root_two_pi * (pre_values + cubic_term)
    tangent = jnp.tanh(inner_arg)
    gelu_value = 0.5 * pre_values * (1.0 + tangent)
    gelu_slope = 0.5 * (1.0 + tangent) + 0.5 * pre_values * (
        1.0 - tangent * tangent
    ) * root_two_pi * (1.0 + 3.0 * gelu_coeff * pre_values * pre_values)
    return (gelu_value, gelu_slope)


def shift(v, axis, step):
    n = lax.axis_size(axis)
    return lax.ppermute(v, axis, [(i, (i + step) % n) for i in range(n)])


def along_z(v, step, senders):
    pairs = [(4 * h + l, (4 * h + l + step) % 8) for h in range(2) for l in senders]
    return lax.ppermute(v, Z, pairs)


def pairs_z(v, steps):
    pairs = [(4 * h + l, (4 * h + l + s) % 8) for h in range(2) for l, s in steps.items()]
    return lax.ppermute(v, Z, pairs)


def at(v, i):
    return lax.dynamic_index_in_dim(v, i, 0, keepdims=False)


def after(v, *first):
    return lax.optimization_barrier((v, *first))[0]


def pack(v):
    top = jnp.max(jnp.abs(v), axis=1, keepdims=True)
    e = jnp.clip(jnp.floor(jnp.log2(jnp.maximum(top, 1e-30))), -100.0, 100.0)
    body = (v * jnp.exp2(13.0 - e)).astype(jnp.float16)
    tail = jnp.broadcast_to(e, (v.shape[0], 128)).astype(jnp.float16)
    return jnp.concatenate([body, tail], axis=1)


def unpack(w):
    n = w.shape[1] - 128
    e = w[:, n : n + 1].astype(jnp.float32)
    return w[:, :n].astype(jnp.float32) * jnp.exp2(e - 13.0)


def on_device(pre_act, grad_out, down_weight):
    y, zh, zl, x, c = (lax.axis_index(a) for a in ("y", "zh", "zl", "x", "core"))
    tokens, hidden = pre_act.shape
    half, feats = grad_out.shape
    block = hidden // 8
    grad_scale = 1.0 / math.sqrt(tokens * 32)

    from_x = [grad_out] + [shift(grad_out, "x", t) for t in (1, 2, 3)]
    p = shift(grad_out, "zh", 1)
    gelu_value, gelu_slope = gelu_parts(pre_act.astype(jnp.float32))
    act, gelu_slope = lax.optimization_barrier((gelu_value.astype(jnp.bfloat16), gelu_slope))
    act = act.reshape(tokens, 4, 2, block).transpose(1, 2, 0, 3)
    act = jnp.where(zh == 1, act[:, ::-1], act)
    halves = act.reshape(4, 2, 2, half, block)
    act = jnp.where(c == 1, halves[:, :, ::-1], halves)
    pieces_out = [at(act, (y + s) % 4) for s in range(4)]
    pieces = [shift(v, "y", s) if s else v for s, v in enumerate(pieces_out)]
    own, cross = (
        jnp.stack([lax.select_n((y - k) % 4, *[v[i] for v in pieces]) for k in range(4)], axis=1)
        for i in range(2)
    )

    both = after(jnp.stack([grad_out, p]), *pieces_out)
    all_rows = lax.all_gather(both, ("x", "y")).reshape(4, 4, 2, half, feats)

    mine = after(jnp.stack(from_x), *pieces_out)
    mine = jnp.stack([mine, shift(mine, "core", 1)], axis=1)

    def partial(*blocks):
        rows = jnp.stack(blocks)
        rows = jnp.where(c == 1, rows[:, ::-1], rows).reshape(-1, feats)
        sums = lax.dot_general(
            rows, down_weight, (((1,), (1,)), ((), ())), preferred_element_type=jnp.float32
        )
        return [sums[k * tokens : (k + 1) * tokens] for k in range(len(blocks))]

    part_far, part_own = partial(*(at(mine, (x - zl - k) % 4) for k in (2, 0)))
    far = after(pack(part_far), own, cross)

    e0, e3 = zl == 0, zl == 3
    far_up = along_z(far, 1, (0, 1))
    far_down = along_z(far, -1, (2, 3))
    a_up = along_z(jnp.where(e3, cross, own), 1, range(4))
    a_down = along_z(jnp.where(e0, cross, own), -1, range(4))
    b = pairs_z(cross, {0: -2, 1: -2, 2: 2, 3: 2})

    q = jnp.where(jnp.where(e0, x == 3, x == 0), p, jnp.zeros_like(p))
    for t in (1, 2, 3):
        q = q + lax.ppermute(p, ("zl", "x"), [(3, (3 + t) % 4), (12, 12 + t)])
    beyond = jnp.stack([q, shift(q, "core", 1)])
    up, down = (at(mine, (x - zl - k) % 4) for k in (1, -1))
    part_up, part_down = partial(jnp.where(e3, beyond, up), jnp.where(e0, beyond, down))

    far_up, far_down, a_up, a_down, b, part_up, part_down = lax.optimization_barrier(
        (far_up, far_down, a_up, a_down, b, part_up, part_down)
    )
    near_up = pack(part_up + unpack(far_up))
    near_down = pack(part_down + unpack(far_down))
    from_below = along_z(near_up, 1, range(4))
    from_above = along_z(near_down, -1, range(4))
    c_up = along_z(jnp.where(e0, b, a_up), 1, (0, 1, 2))
    c_down = along_z(jnp.where(e3, b, a_down), -1, (3, 2, 1))
    d = pairs_z(b, {1: 1, 2: -1})

    c_up, c_down, d = lax.optimization_barrier((c_up, c_down, d, near_up, near_down))[:3]
    e = pairs_z(jnp.where(zl == 1, c_up, c_down), {1: 1, 2: -1})
    f = pairs_z(jnp.where(zl == 2, c_up, c_down), {1: -1, 2: 1})
    g = pairs_z(d, {1: -1, 2: 1})

    e, f, g, all_rows = lax.optimization_barrier((e, f, g, all_rows))
    h = pairs_z(e, {1: -1, 2: 1})
    other_rows = shift(all_rows, "core", 1)

    def choose(*units):
        return lax.select_n(zl, *units)

    in_group = (
        choose(own, a_up, c_up, f),
        choose(a_down, own, a_up, c_up),
        choose(c_down, a_down, own, a_up),
        choose(f, c_down, a_down, own),
    )
    from_group = (
        choose(g, d, b, a_down),
        choose(h, e, c_down, b),
        choose(b, c_up, e, h),
        choose(a_up, b, d, g),
    )
    none = jnp.zeros_like(own)
    early = (from_group[0], choose(none, e, c_down, b), choose(b, c_up, e, none), from_group[3])
    last = choose(h, none, none, h)

    def product(core, first, second, rows):
        unit = jnp.stack([jnp.stack([i[core], j[core]], axis=1) for i, j in zip(first, second)])
        return lax.dot_general(
            unit.reshape(-1, block), rows.reshape(-1, feats), (((0,), (0,)), ((), ())),
            preferred_element_type=jnp.float32,
        )

    summed = product(0, in_group, early, all_rows)
    from_below, from_above = after(from_below, summed), after(from_above, summed)
    summed += product(0, (none,), (last,), at(all_rows, jnp.where(zl < 2, 1, 2)))
    summed += product(1, in_group, from_group, other_rows)

    grad_act = part_own + unpack(from_below) + unpack(from_above)
    grad_pre = (grad_act * gelu_slope).astype(jnp.bfloat16)
    return (grad_pre, summed * grad_scale)


def solution(mesh):
    axes = ("y", "zh", "zl", "x", "core")
    fine = Mesh(mesh.devices.reshape(4, 2, 4, 4, 2), axes)
    dp, row, col = ("y", "zh"), "zl", ("x", "core")
    return jax.shard_map(
        on_device,
        mesh=fine,
        in_specs=(P((*dp, row), col), P((*dp, *col), row), P(col, row)),
        out_specs=(P((*dp, row), col), P((*col, *dp), row)),
        check_vma=False,
    )
```

```python
import math

import jax
import jax.numpy as jnp
from jax import lax
from jax.sharding import Mesh
from jax.sharding import PartitionSpec as P

root_two_pi = math.sqrt(2.0 / math.pi)
gelu_coeff = 0.044715
Z = ("zh", "zl")


def gelu_parts(pre_values):
    cubic_term = gelu_coeff * pre_values * pre_values * pre_values
    inner_arg = root_two_pi * (pre_values + cubic_term)
    tangent = jnp.tanh(inner_arg)
    gelu_value = 0.5 * pre_values * (1.0 + tangent)
    gelu_slope = 0.5 * (1.0 + tangent) + 0.5 * pre_values * (
        1.0 - tangent * tangent
    ) * root_two_pi * (1.0 + 3.0 * gelu_coeff * pre_values * pre_values)
    return (gelu_value, gelu_slope)


def shift(v, axis, step):
    n = lax.axis_size(axis)
    return lax.ppermute(v, axis, [(i, (i + step) % n) for i in range(n)])


def along_z(v, step, senders):
    pairs = [(4 * h + l, (4 * h + l + step) % 8) for h in range(2) for l in senders]
    return lax.ppermute(v, Z, pairs)


def pairs_z(v, steps):
    pairs = [(4 * h + l, (4 * h + l + s) % 8) for h in range(2) for l, s in steps.items()]
    return lax.ppermute(v, Z, pairs)


def at(v, i):
    return lax.dynamic_index_in_dim(v, i, 0, keepdims=False)


def after(v, *first):
    return lax.optimization_barrier((v, *first))[0]


def pack(v):
    top = jnp.max(jnp.abs(v), axis=1, keepdims=True)
    e = jnp.clip(jnp.floor(jnp.log2(jnp.maximum(top, 1e-30))), -100.0, 100.0)
    body = (v * jnp.exp2(13.0 - e)).astype(jnp.float16)
    tail = jnp.broadcast_to(e, (v.shape[0], 128)).astype(jnp.float16)
    return jnp.concatenate([body, tail], axis=1)


def unpack(w):
    n = w.shape[1] - 128
    e = w[:, n : n + 1].astype(jnp.float32)
    return w[:, :n].astype(jnp.float32) * jnp.exp2(e - 13.0)


def on_device(pre_act, grad_out, down_weight):
    y, zh, zl, x, c = (lax.axis_index(a) for a in ("y", "zh", "zl", "x", "core"))
    tokens, hidden = pre_act.shape
    half, feats = grad_out.shape
    block = hidden // 8
    grad_scale = 1.0 / math.sqrt(tokens * 32)

    gelu_value, gelu_slope = gelu_parts(pre_act.astype(jnp.float32))
    act, gelu_slope = lax.optimization_barrier((gelu_value.astype(jnp.bfloat16), gelu_slope))
    act = act.reshape(tokens, 4, 2, block).transpose(1, 2, 0, 3)
    act = jnp.where(zh == 1, act[:, ::-1], act)
    halves = act.reshape(4, 2, 2, half, block)
    act = jnp.where(c == 1, halves[:, :, ::-1], halves)
    pieces_out = [at(act, (y + s) % 4) for s in range(4)]
    pieces = [shift(v, "y", s) if s else v for s, v in enumerate(pieces_out)]
    grad_out = after(grad_out, *pieces_out)
    p = shift(grad_out, "zh", 1)
    from_x = [grad_out] + [shift(grad_out, "x", t) for t in (1, 2, 3)]
    own, cross = (
        jnp.stack([lax.select_n((y - k) % 4, *[v[i] for v in pieces]) for k in range(4)], axis=1)
        for i in range(2)
    )

    both = jnp.stack([grad_out, p])
    all_rows = lax.all_gather(both, ("x", "y")).reshape(4, 4, 2, half, feats)

    mine = jnp.stack(from_x)
    mine = jnp.stack([mine, shift(mine, "core", 1)], axis=1)

    def partial(*blocks):
        rows = jnp.stack(blocks)
        rows = jnp.where(c == 1, rows[:, ::-1], rows).reshape(-1, feats)
        sums = lax.dot_general(
            rows, down_weight, (((1,), (1,)), ((), ())), preferred_element_type=jnp.float32
        )
        return [sums[k * tokens : (k + 1) * tokens] for k in range(len(blocks))]

    part_far, part_own = partial(*(at(mine, (x - zl - k) % 4) for k in (2, 0)))
    far = after(pack(part_far), own, cross)

    e0, e3 = zl == 0, zl == 3
    far_up = along_z(far, 1, (0, 1))
    far_down = along_z(far, -1, (2, 3))
    a_up = along_z(jnp.where(e3, cross, own), 1, range(4))
    a_down = along_z(jnp.where(e0, cross, own), -1, range(4))
    b = pairs_z(cross, {0: -2, 1: -2, 2: 2, 3: 2})

    q = jnp.where(jnp.where(e0, x == 3, x == 0), p, jnp.zeros_like(p))
    for t in (1, 2, 3):
        q = q + lax.ppermute(p, ("zl", "x"), [(3, (3 + t) % 4), (12, 12 + t)])
    beyond = jnp.stack([q, shift(q, "core", 1)])
    up, down = (at(mine, (x - zl - k) % 4) for k in (1, -1))
    part_up, part_down = partial(jnp.where(e3, beyond, up), jnp.where(e0, beyond, down))

    far_up, far_down, a_up, a_down, b, part_up, part_down = lax.optimization_barrier(
        (far_up, far_down, a_up, a_down, b, part_up, part_down)
    )
    near_up = pack(part_up + unpack(far_up))
    near_down = pack(part_down + unpack(far_down))
    from_below = along_z(near_up, 1, range(4))
    from_above = along_z(near_down, -1, range(4))
    c_up = along_z(jnp.where(e0, b, a_up), 1, (0, 1, 2))
    c_down = along_z(jnp.where(e3, b, a_down), -1, (3, 2, 1))
    d = pairs_z(b, {1: 1, 2: -1})

    c_up, c_down, d = lax.optimization_barrier((c_up, c_down, d, near_up, near_down))[:3]
    e = pairs_z(jnp.where(zl == 1, c_up, c_down), {1: 1, 2: -1})
    f = pairs_z(jnp.where(zl == 2, c_up, c_down), {1: -1, 2: 1})
    g = pairs_z(d, {1: -1, 2: 1})

    e, f, g, all_rows = lax.optimization_barrier((e, f, g, all_rows))
    h = pairs_z(e, {1: -1, 2: 1})
    other_rows = shift(all_rows, "core", 1)

    def choose(*units):
        return lax.select_n(zl, *units)

    none = jnp.zeros_like(own)
    in_group = (
        choose(own, a_up, c_up, f),
        choose(a_down, own, a_up, c_up),
        choose(c_down, a_down, own, a_up),
        choose(f, c_down, a_down, own),
    )
    from_group = (
        choose(g, d, b, a_down),
        choose(none, e, c_down, b),
        choose(b, c_up, e, none),
        choose(a_up, b, d, g),
    )
    units = lax.optimization_barrier(
        [
            jnp.stack([jnp.stack([i[core], k[core]], axis=1) for i, k in zip(in_group, from_group)])
            for core in range(2)
        ]
    )

    def product(unit, rows):
        return lax.dot_general(
            unit.reshape(-1, block), rows.reshape(-1, feats), (((0,), (0,)), ((), ())),
            preferred_element_type=jnp.float32,
        )

    late = jnp.where(zl < 2, 1, 2)
    summed = product(units[0], all_rows)
    other_rows = after(other_rows, summed)
    late_rows = jnp.stack([at(all_rows, late)[:, 1], at(other_rows, late)[:, 1]])
    summed += product(units[1], other_rows)
    from_below, from_above = after(from_below, summed), after(from_above, summed)
    summed += product(h, late_rows)

    grad_act = part_own + unpack(from_below) + unpack(from_above)
    grad_pre = (grad_act * gelu_slope).astype(jnp.bfloat16)
    return (grad_pre, summed * grad_scale)


def solution(mesh):
    axes = ("y", "zh", "zl", "x", "core")
    fine = Mesh(mesh.devices.reshape(4, 2, 4, 4, 2), axes)
    dp, row, col = ("y", "zh"), "zl", ("x", "core")
    return jax.shard_map(
        on_device,
        mesh=fine,
        in_specs=(P((*dp, row), col), P((*dp, *col), row), P(col, row)),
        out_specs=(P((*dp, row), col), P((*col, *dp), row)),
        check_vma=False,
    )
```

```python
import math

import jax
import jax.numpy as jnp
from jax import lax
from jax.sharding import Mesh
from jax.sharding import PartitionSpec as P

root_two_pi = math.sqrt(2.0 / math.pi)
gelu_coeff = 0.044715
Z = ("zh", "zl")


def gelu_parts(pre_values):
    cubic_term = gelu_coeff * pre_values * pre_values * pre_values
    inner_arg = root_two_pi * (pre_values + cubic_term)
    tangent = jnp.tanh(inner_arg)
    gelu_value = 0.5 * pre_values * (1.0 + tangent)
    gelu_slope = 0.5 * (1.0 + tangent) + 0.5 * pre_values * (
        1.0 - tangent * tangent
    ) * root_two_pi * (1.0 + 3.0 * gelu_coeff * pre_values * pre_values)
    return (gelu_value, gelu_slope)


def shift(v, axis, step):
    n = lax.axis_size(axis)
    return lax.ppermute(v, axis, [(i, (i + step) % n) for i in range(n)])


def along_z(v, step, senders):
    pairs = [(4 * h + l, (4 * h + l + step) % 8) for h in range(2) for l in senders]
    return lax.ppermute(v, Z, pairs)


def pairs_z(v, steps):
    pairs = [(4 * h + l, (4 * h + l + s) % 8) for h in range(2) for l, s in steps.items()]
    return lax.ppermute(v, Z, pairs)


def at(v, i):
    return lax.dynamic_index_in_dim(v, i, 0, keepdims=False)


def after(v, *first):
    return lax.optimization_barrier((v, *first))[0]


def pack(v):
    top = jnp.max(jnp.abs(v), axis=1, keepdims=True)
    e = jnp.clip(jnp.floor(jnp.log2(jnp.maximum(top, 1e-30))), -100.0, 100.0)
    body = (v * jnp.exp2(13.0 - e)).astype(jnp.float16)
    tail = jnp.broadcast_to(e, (v.shape[0], 128)).astype(jnp.float16)
    return jnp.concatenate([body, tail], axis=1)


def unpack(w):
    n = w.shape[1] - 128
    e = w[:, n : n + 1].astype(jnp.float32)
    return w[:, :n].astype(jnp.float32) * jnp.exp2(e - 13.0)


def on_device(pre_act, grad_out, down_weight):
    y, zh, zl, x, c = (lax.axis_index(a) for a in ("y", "zh", "zl", "x", "core"))
    tokens, hidden = pre_act.shape
    half, feats = grad_out.shape
    block = hidden // 8
    grad_scale = 1.0 / math.sqrt(tokens * 32)

    e0, e3 = zl == 0, zl == 3
    p = shift(grad_out, "zh", 1)

    gelu_value, gelu_slope = gelu_parts(pre_act.astype(jnp.float32))
    act, gelu_slope = lax.optimization_barrier((gelu_value.astype(jnp.bfloat16), gelu_slope))
    act = act.reshape(tokens, 4, 2, block).transpose(1, 2, 0, 3)
    act = jnp.where(zh == 1, act[:, ::-1], act)
    halves = act.reshape(4, 2, 2, half, block)
    act = jnp.where(c == 1, halves[:, :, ::-1], halves)
    pieces_out = [at(act, (y + s) % 4) for s in range(4)]
    pieces = [shift(v, "y", s) if s else v for s, v in enumerate(pieces_out)]
    own, cross = (
        jnp.stack([lax.select_n((y - k) % 4, *[v[i] for v in pieces]) for k in range(4)], axis=1)
        for i in range(2)
    )

    both = after(jnp.stack([grad_out, p]), own, cross)
    all_rows = lax.all_gather(both, ("x", "y")).reshape(4, 4, 2, half, feats)

    a_up = along_z(jnp.where(e3, cross, own), 1, range(4))
    a_down = along_z(jnp.where(e0, cross, own), -1, range(4))
    b = pairs_z(cross, {0: -2, 1: -2, 2: 2, 3: 2})

    near_g = after(grad_out, own, cross)
    from_x = [near_g] + [shift(near_g, "x", t) for t in (1, 2, 3)]
    p, *from_x = lax.optimization_barrier((p, *from_x, a_up, a_down))[:5]
    beyond = jnp.where(jnp.where(e0, x == 3, x == 0), p, jnp.zeros_like(p))
    for t in (1, 2, 3):
        beyond = beyond + lax.ppermute(p, ("zl", "x"), [(3, (3 + t) % 4), (12, 12 + t)])
    mine = jnp.stack(from_x + [beyond])
    mine = jnp.stack([mine, shift(mine, "core", 1)], axis=1)

    place = [(x - zl - k) % 4 for k in (2, 1, -1, 0)]
    place[1] = jnp.where(e3, 4, place[1])
    place[2] = jnp.where(e0, 4, place[2])
    rows = jnp.stack([at(mine, k) for k in place])
    rows = jnp.where(c == 1, rows[:, ::-1], rows).reshape(4 * tokens, feats)
    parts = lax.dot_general(
        rows, down_weight, (((1,), (1,)), ((), ())), preferred_element_type=jnp.float32
    )
    part_far, part_up, part_down, part_own = (
        parts[k * tokens : (k + 1) * tokens] for k in range(4)
    )
    far = pack(part_far)

    far_up = along_z(far, 1, (0, 1))
    far_down = along_z(far, -1, (2, 3))
    c_up = along_z(jnp.where(e0, b, a_up), 1, (0, 1, 2))
    c_down = along_z(jnp.where(e3, b, a_down), -1, (3, 2, 1))
    d = pairs_z(b, {1: 1, 2: -1})
    c_up, c_down, d = lax.optimization_barrier((c_up, c_down, d))
    e = pairs_z(jnp.where(zl == 1, c_up, c_down), {1: 1, 2: -1})
    f = pairs_z(jnp.where(zl == 2, c_up, c_down), {1: -1, 2: 1})
    g = pairs_z(d, {1: -1, 2: 1})
    e, f, g, far = lax.optimization_barrier((e, f, g, far))
    h = pairs_z(e, {1: -1, 2: 1})
    far_up, far_down = lax.optimization_barrier((far_up, far_down, e, f, g))[:2]
    near_up = pack(part_up + unpack(far_up))
    near_down = pack(part_down + unpack(far_down))
    from_below = along_z(near_up, 1, range(4))
    from_above = along_z(near_down, -1, range(4))
    other_rows = shift(after(all_rows, e, f, g), "core", 1)

    def choose(*units):
        return lax.select_n(zl, *units)

    in_group = (
        choose(own, a_up, c_up, f),
        choose(a_down, own, a_up, c_up),
        choose(c_down, a_down, own, a_up),
        choose(f, c_down, a_down, own),
    )
    from_group = (
        choose(g, d, b, a_down),
        choose(h, e, c_down, b),
        choose(b, c_up, e, h),
        choose(a_up, b, d, g),
    )
    units = lax.optimization_barrier(
        [
            jnp.stack([jnp.stack([i[core], k[core]], axis=1) for i, k in zip(in_group, from_group)])
            for core in range(2)
        ]
    )

    def product(unit, rows):
        return lax.dot_general(
            unit.reshape(-1, block), rows.reshape(-1, feats), (((0,), (0,)), ((), ())),
            preferred_element_type=jnp.float32,
        )

    summed = product(units[0], all_rows)
    summed += product(units[1], after(other_rows, summed))
    from_below, from_above = lax.optimization_barrier((from_below, from_above, summed))[:2]

    grad_act = part_own + unpack(from_below) + unpack(from_above)
    grad_pre = (grad_act * gelu_slope).astype(jnp.bfloat16)
    return (grad_pre, summed * grad_scale)


def solution(mesh):
    axes = ("y", "zh", "zl", "x", "core")
    fine = Mesh(mesh.devices.reshape(4, 2, 4, 4, 2), axes)
    dp, row, col = ("y", "zh"), "zl", ("x", "core")
    return jax.shard_map(
        on_device,
        mesh=fine,
        in_specs=(P((*dp, row), col), P((*dp, *col), row), P(col, row)),
        out_specs=(P((*dp, row), col), P((*col, *dp), row)),
        check_vma=False,
    )
```

```python
import math

import jax
import jax.numpy as jnp
from jax import lax
from jax.sharding import Mesh
from jax.sharding import PartitionSpec as P

root_two_pi = math.sqrt(2.0 / math.pi)
gelu_coeff = 0.044715
Z = ("zh", "zl")


def gelu_parts(pre_values):
    cubic_term = gelu_coeff * pre_values * pre_values * pre_values
    inner_arg = root_two_pi * (pre_values + cubic_term)
    tangent = jnp.tanh(inner_arg)
    gelu_value = 0.5 * pre_values * (1.0 + tangent)
    gelu_slope = 0.5 * (1.0 + tangent) + 0.5 * pre_values * (
        1.0 - tangent * tangent
    ) * root_two_pi * (1.0 + 3.0 * gelu_coeff * pre_values * pre_values)
    return (gelu_value, gelu_slope)


def shift(v, axis, step):
    n = lax.axis_size(axis)
    return lax.ppermute(v, axis, [(i, (i + step) % n) for i in range(n)])


def along_z(v, step, senders):
    pairs = [(4 * h + l, (4 * h + l + step) % 8) for h in range(2) for l in senders]
    return lax.ppermute(v, Z, pairs)


def pairs_z(v, steps):
    pairs = [(4 * h + l, (4 * h + l + s) % 8) for h in range(2) for l, s in steps.items()]
    return lax.ppermute(v, Z, pairs)


def at(v, i):
    return lax.dynamic_index_in_dim(v, i, 0, keepdims=False)


def after(v, *first):
    return lax.optimization_barrier((v, *first))[0]


def pack(v):
    top = jnp.max(jnp.abs(v), axis=1, keepdims=True)
    e = jnp.clip(jnp.floor(jnp.log2(jnp.maximum(top, 1e-30))), -100.0, 100.0)
    body = (v * jnp.exp2(13.0 - e)).astype(jnp.float16)
    tail = jnp.broadcast_to(e, (v.shape[0], 128)).astype(jnp.float16)
    return jnp.concatenate([body, tail], axis=1)


def unpack(w):
    n = w.shape[1] - 128
    e = w[:, n : n + 1].astype(jnp.float32)
    return w[:, :n].astype(jnp.float32) * jnp.exp2(e - 13.0)


def on_device(pre_act, grad_out, down_weight):
    y, zh, zl, x, c = (lax.axis_index(a) for a in ("y", "zh", "zl", "x", "core"))
    tokens, hidden = pre_act.shape
    half, feats = grad_out.shape
    block = hidden // 8
    grad_scale = 1.0 / math.sqrt(tokens * 32)

    e0, e3 = zl == 0, zl == 3
    p = shift(grad_out, "zh", 1)

    gelu_value, gelu_slope = gelu_parts(pre_act.astype(jnp.float32))
    act, gelu_slope = lax.optimization_barrier((gelu_value.astype(jnp.bfloat16), gelu_slope))
    act = act.reshape(tokens, 4, 2, block).transpose(1, 2, 0, 3)
    act = jnp.where(zh == 1, act[:, ::-1], act)
    halves = act.reshape(4, 2, 2, half, block)
    act = jnp.where(c == 1, halves[:, :, ::-1], halves)
    pieces_out = [at(act, (y + s) % 4) for s in range(4)]
    pieces = [shift(v, "y", s) if s else v for s, v in enumerate(pieces_out)]
    own, cross = (
        jnp.stack([lax.select_n((y - k) % 4, *[v[i] for v in pieces]) for k in range(4)], axis=1)
        for i in range(2)
    )

    both = after(jnp.stack([grad_out, p]), own, cross)
    all_rows = lax.all_gather(both, ("x", "y")).reshape(4, 4, 2, half, feats)

    a_up = along_z(jnp.where(e3, cross, own), 1, range(4))
    a_down = along_z(jnp.where(e0, cross, own), -1, range(4))
    b = pairs_z(cross, {0: -2, 1: -2, 2: 2, 3: 2})

    near_g = after(grad_out, own, cross)
    from_x = [near_g] + [shift(near_g, "x", t) for t in (1, 2, 3)]
    from_x = lax.optimization_barrier((*from_x, a_up, a_down, b))[:4]
    mine = jnp.stack(from_x)
    mine = jnp.stack([mine, shift(mine, "core", 1)], axis=1)

    def partial(*blocks):
        rows = jnp.stack(blocks)
        rows = jnp.where(c == 1, rows[:, ::-1], rows).reshape(-1, feats)
        sums = lax.dot_general(
            rows, down_weight, (((1,), (1,)), ((), ())), preferred_element_type=jnp.float32
        )
        return [sums[k * tokens : (k + 1) * tokens] for k in range(len(blocks))]

    part_far, part_own = partial(*(at(mine, (x - zl - k) % 4) for k in (2, 0)))
    far = pack(part_far)
    p = after(p, far)
    beyond = jnp.where(jnp.where(e0, x == 3, x == 0), p, jnp.zeros_like(p))
    for t in (1, 2, 3):
        beyond = beyond + lax.ppermute(p, ("zl", "x"), [(3, (3 + t) % 4), (12, 12 + t)])
    beyond = jnp.stack([beyond, shift(beyond, "core", 1)])
    up, down = (at(mine, (x - zl - k) % 4) for k in (1, -1))
    part_up, part_down = partial(jnp.where(e3, beyond, up), jnp.where(e0, beyond, down))

    far_up = along_z(far, 1, (0, 1))
    far_down = along_z(far, -1, (2, 3))
    c_up = along_z(jnp.where(e0, b, a_up), 1, (0, 1, 2))
    c_down = along_z(jnp.where(e3, b, a_down), -1, (3, 2, 1))
    d = pairs_z(b, {1: 1, 2: -1})
    c_up, c_down, d = lax.optimization_barrier((c_up, c_down, d, far))[:3]
    e = pairs_z(jnp.where(zl == 1, c_up, c_down), {1: 1, 2: -1})
    f = pairs_z(jnp.where(zl == 2, c_up, c_down), {1: -1, 2: 1})
    g = pairs_z(d, {1: -1, 2: 1})
    e, f, g = lax.optimization_barrier((e, f, g))
    h = pairs_z(e, {1: -1, 2: 1})
    far_up, far_down = lax.optimization_barrier((far_up, far_down, g))[:2]
    near_up = pack(part_up + unpack(far_up))
    near_down = pack(part_down + unpack(far_down))
    from_below = along_z(near_up, 1, range(4))
    from_above = along_z(near_down, -1, range(4))
    h = after(h, near_up, near_down)
    other_rows = shift(after(all_rows, e, f, g), "core", 1)

    def choose(*units):
        return lax.select_n(zl, *units)

    in_group = (
        choose(own, a_up, c_up, f),
        choose(a_down, own, a_up, c_up),
        choose(c_down, a_down, own, a_up),
        choose(f, c_down, a_down, own),
    )
    from_group = (
        choose(g, d, b, a_down),
        choose(h, e, c_down, b),
        choose(b, c_up, e, h),
        choose(a_up, b, d, g),
    )
    units = lax.optimization_barrier(
        [
            jnp.stack([jnp.stack([i[core], k[core]], axis=1) for i, k in zip(in_group, from_group)])
            for core in range(2)
        ]
    )

    def product(unit, rows):
        return lax.dot_general(
            unit.reshape(-1, block), rows.reshape(-1, feats), (((0,), (0,)), ((), ())),
            preferred_element_type=jnp.float32,
        )

    summed = product(units[0], all_rows)
    summed += product(units[1], after(other_rows, summed))
    from_below, from_above = lax.optimization_barrier((from_below, from_above, summed))[:2]

    grad_act = part_own + unpack(from_below) + unpack(from_above)
    grad_pre = (grad_act * gelu_slope).astype(jnp.bfloat16)
    return (grad_pre, summed * grad_scale)


def solution(mesh):
    axes = ("y", "zh", "zl", "x", "core")
    fine = Mesh(mesh.devices.reshape(4, 2, 4, 4, 2), axes)
    dp, row, col = ("y", "zh"), "zl", ("x", "core")
    return jax.shard_map(
        on_device,
        mesh=fine,
        in_specs=(P((*dp, row), col), P((*dp, *col), row), P(col, row)),
        out_specs=(P((*dp, row), col), P((*col, *dp), row)),
        check_vma=False,
    )
```

```python
import math

import jax
import jax.numpy as jnp
from jax import lax
from jax.sharding import Mesh
from jax.sharding import PartitionSpec as P

root_two_pi = math.sqrt(2.0 / math.pi)
gelu_coeff = 0.044715
Z = ("zh", "zl")


def gelu_parts(pre_values):
    cubic_term = gelu_coeff * pre_values * pre_values * pre_values
    inner_arg = root_two_pi * (pre_values + cubic_term)
    tangent = jnp.tanh(inner_arg)
    gelu_value = 0.5 * pre_values * (1.0 + tangent)
    gelu_slope = 0.5 * (1.0 + tangent) + 0.5 * pre_values * (
        1.0 - tangent * tangent
    ) * root_two_pi * (1.0 + 3.0 * gelu_coeff * pre_values * pre_values)
    return (gelu_value, gelu_slope)


def shift(v, axis, step):
    n = lax.axis_size(axis)
    return lax.ppermute(v, axis, [(i, (i + step) % n) for i in range(n)])


def along_z(v, step, senders):
    pairs = [(4 * h + l, (4 * h + l + step) % 8) for h in range(2) for l in senders]
    return lax.ppermute(v, Z, pairs)


def pairs_z(v, steps):
    pairs = [(4 * h + l, (4 * h + l + s) % 8) for h in range(2) for l, s in steps.items()]
    return lax.ppermute(v, Z, pairs)


def at(v, i):
    return lax.dynamic_index_in_dim(v, i, 0, keepdims=False)


def after(v, *first):
    return lax.optimization_barrier((v, *first))[0]


def pack(v):
    top = jnp.max(jnp.abs(v), axis=1, keepdims=True)
    e = jnp.clip(jnp.floor(jnp.log2(jnp.maximum(top, 1e-30))), -100.0, 100.0)
    body = (v * jnp.exp2(13.0 - e)).astype(jnp.float16)
    tail = jnp.broadcast_to(e, (v.shape[0], 128)).astype(jnp.float16)
    return jnp.concatenate([body, tail], axis=1)


def unpack(w):
    n = w.shape[1] - 128
    e = w[:, n : n + 1].astype(jnp.float32)
    return w[:, :n].astype(jnp.float32) * jnp.exp2(e - 13.0)


def on_device(pre_act, grad_out, down_weight):
    y, zh, zl, x, c = (lax.axis_index(a) for a in ("y", "zh", "zl", "x", "core"))
    tokens, hidden = pre_act.shape
    half, feats = grad_out.shape
    block = hidden // 8
    grad_scale = 1.0 / math.sqrt(tokens * 32)

    e0, e3 = zl == 0, zl == 3
    p = shift(grad_out, "zh", 1)

    gelu_value, gelu_slope = gelu_parts(pre_act.astype(jnp.float32))
    act, gelu_slope = lax.optimization_barrier((gelu_value.astype(jnp.bfloat16), gelu_slope))
    act = act.reshape(tokens, 4, 2, block).transpose(1, 2, 0, 3)
    act = jnp.where(zh == 1, act[:, ::-1], act)
    halves = act.reshape(4, 2, 2, half, block)
    act = jnp.where(c == 1, halves[:, :, ::-1], halves)
    pieces_out = [at(act, (y + s) % 4) for s in range(4)]
    pieces = [shift(v, "y", s) if s else v for s, v in enumerate(pieces_out)]
    own, cross = (
        jnp.stack([lax.select_n((y - k) % 4, *[v[i] for v in pieces]) for k in range(4)], axis=1)
        for i in range(2)
    )

    both = after(jnp.stack([grad_out, p]), own, cross)
    all_rows = lax.all_gather(both, ("x", "y")).reshape(4, 4, 2, half, feats)

    a_up = along_z(jnp.where(e3, cross, own), 1, range(4))
    a_down = along_z(jnp.where(e0, cross, own), -1, range(4))
    b = pairs_z(cross, {0: -2, 1: -2, 2: 2, 3: 2})

    near_g = after(grad_out, own, cross)
    from_x = [near_g] + [shift(near_g, "x", t) for t in (1, 2, 3)]
    from_x = lax.optimization_barrier((*from_x, a_up, a_down, b))[:4]
    mine = jnp.stack(from_x)
    mine = jnp.stack([mine, shift(mine, "core", 1)], axis=1)

    def partial(*blocks):
        rows = jnp.stack(blocks)
        rows = jnp.where(c == 1, rows[:, ::-1], rows).reshape(-1, feats)
        sums = lax.dot_general(
            rows, down_weight, (((1,), (1,)), ((), ())), preferred_element_type=jnp.float32
        )
        return [sums[k * tokens : (k + 1) * tokens] for k in range(len(blocks))]

    part_far, part_own = partial(*(at(mine, (x - zl - k) % 4) for k in (2, 0)))
    far = pack(part_far)
    p = after(p, far)
    beyond = jnp.where(jnp.where(e0, x == 3, x == 0), p, jnp.zeros_like(p))
    for t in (1, 2, 3):
        beyond = beyond + lax.ppermute(p, ("zl", "x"), [(3, (3 + t) % 4), (12, 12 + t)])
    beyond = jnp.stack([beyond, shift(beyond, "core", 1)])
    up, down = (at(mine, (x - zl - k) % 4) for k in (1, -1))
    part_up, part_down = partial(jnp.where(e3, beyond, up), jnp.where(e0, beyond, down))

    far_up = along_z(far, 1, (0, 1))
    far_down = along_z(far, -1, (2, 3))
    c_up = along_z(jnp.where(e0, b, a_up), 1, (0, 1, 2))
    c_down = along_z(jnp.where(e3, b, a_down), -1, (3, 2, 1))
    d = pairs_z(b, {1: 1, 2: -1})
    c_up, c_down, d = lax.optimization_barrier((c_up, c_down, d, far))[:3]
    e = pairs_z(jnp.where(zl == 1, c_up, c_down), {1: 1, 2: -1})
    f = pairs_z(jnp.where(zl == 2, c_up, c_down), {1: -1, 2: 1})
    g = pairs_z(d, {1: -1, 2: 1})
    e, f, g, part_up, part_down = lax.optimization_barrier((e, f, g, part_up, part_down))
    h = pairs_z(e, {1: -1, 2: 1})
    far_up, far_down = lax.optimization_barrier((far_up, far_down, g))[:2]
    near_up = pack(part_up + unpack(far_up))
    near_down = pack(part_down + unpack(far_down))
    from_below = along_z(near_up, 1, range(4))
    from_above = along_z(near_down, -1, range(4))
    h = after(h, near_up, near_down)
    own = after(own, near_up, near_down)
    other_rows = shift(after(all_rows, e, f, g), "core", 1)

    def choose(*units):
        return lax.select_n(zl, *units)

    in_group = (
        choose(own, a_up, c_up, f),
        choose(a_down, own, a_up, c_up),
        choose(c_down, a_down, own, a_up),
        choose(f, c_down, a_down, own),
    )
    from_group = (
        choose(g, d, b, a_down),
        choose(h, e, c_down, b),
        choose(b, c_up, e, h),
        choose(a_up, b, d, g),
    )
    units = lax.optimization_barrier(
        [
            jnp.stack([jnp.stack([i[core], k[core]], axis=1) for i, k in zip(in_group, from_group)])
            for core in range(2)
        ]
    )

    def product(unit, rows):
        return lax.dot_general(
            unit.reshape(-1, block), rows.reshape(-1, feats), (((0,), (0,)), ((), ())),
            preferred_element_type=jnp.float32,
        )

    summed = product(units[0], all_rows)
    summed += product(units[1], after(other_rows, summed))
    from_below, from_above = lax.optimization_barrier((from_below, from_above, summed))[:2]

    grad_act = part_own + unpack(from_below) + unpack(from_above)
    grad_pre = (grad_act * gelu_slope).astype(jnp.bfloat16)
    return (grad_pre, summed * grad_scale)


def solution(mesh):
    axes = ("y", "zh", "zl", "x", "core")
    fine = Mesh(mesh.devices.reshape(4, 2, 4, 4, 2), axes)
    dp, row, col = ("y", "zh"), "zl", ("x", "core")
    return jax.shard_map(
        on_device,
        mesh=fine,
        in_specs=(P((*dp, row), col), P((*dp, *col), row), P(col, row)),
        out_specs=(P((*dp, row), col), P((*col, *dp), row)),
        check_vma=False,
    )
```
